256 devices in a mesh: dp: 32 (over y, x, core), mp: 8 (over z).
Axes of the slice: x: 4, y: 4, z: 8, core: 2. Of those that a mesh axis runs over, the one named last changes fastest.
Arguments:
- acts: bfloat16 [128, 256, 18432], P('dp', None, 'mp'), may hold values from -60 to 60
- out_grads: bfloat16 [128, 256, 2304], P('dp', None, 'mp'), may hold values from -60 to 60
Outputs:
- grad_mean: float32 [2304, 18432], P('dp', 'mp')
- clip_factor: float32 [128], P('dp')
The draws below stay inside these ranges and needn't reach their ends.
All inputs are finite; a program needn't handle non-finite values.
Results may differ from the reference program's by a relative error of at most 0.002.
Values may be sent and summed in bfloat16 or wider, within the bound.
A program may use at most 128 MiB of HBM per device.

```python
import math
import jax
import jax.numpy as jnp
from jax import lax

D = 2304
F = 18432
SEQ = 256
EX_DEV = 4
EXAMPLES = 128
N_DP = 32


def spread_factor(key, shape):
    unit = jax.random.uniform(key, shape, jnp.float32)
    return jnp.exp((unit * 2.0 - 1.0) * math.log(10.0 ** 0.5)) / 1.466


def scaled_field(key, width):
    keys = jax.random.split(key, 5)
    example_scale = jnp.exp(jax.random.uniform(keys[0], (EXAMPLES, 1, 1), jnp.float32, -math.log(2.0), math.log(2.0)))
    token_scale = spread_factor(keys[1], (EXAMPLES, SEQ, 1))
    rising = jnp.sqrt(0.5 + jnp.arange(width, dtype=jnp.float32) / width)
    column_scale = spread_factor(keys[2], (1, 1, width)) * rising[None, None, :]
    return (example_scale * token_scale * column_scale, keys[3], keys[4])


def shared_part(key, width, weight):
    return weight * jax.random.normal(key, (EXAMPLES, 1, width), jnp.float32)


def draw_acts(key, part):
    key = jax.random.fold_in(key, 11)
    scales, base_key, common_key = scaled_field(key, F)
    base = jax.random.normal(base_key, (EXAMPLES, SEQ, F), jnp.float32)
    base = base + shared_part(common_key, F, 0.3)
    return jnp.clip(scales * base, -60.0, 60.0).astype(jnp.bfloat16)


def draw_out_grads(key, part):
    key = jax.random.fold_in(key, 23)
    scales, base_key, common_key = scaled_field(key, D)
    base = jax.random.normal(base_key, (EXAMPLES, SEQ, D), jnp.float32)
    base = base + shared_part(common_key, D, 0.3)
    return jnp.clip(scales * base, -60.0, 60.0).astype(jnp.bfloat16)


def setup_inputs(seed: int = 0) -> dict:
    seeds = jax.random.split(jax.random.key(seed), 3)
    return {
        "acts": draw_acts(jax.random.fold_in(seeds[2], 71), 0),
        "out_grads": draw_out_grads(jax.random.fold_in(seeds[2], 71), 0),
    }


def reference(acts, out_grads):
    bound = math.sqrt(F * D * SEQ)

    def norm_of(pair):
        left, right = pair
        act_gram = jnp.dot(left, left.T, preferred_element_type=jnp.float32)
        grad_gram = jnp.dot(right, right.T, preferred_element_type=jnp.float32)
        return jnp.sum(act_gram * grad_gram)
    sq_norm = lax.map(norm_of, (acts, out_grads))
    clip_factor = bound / jnp.maximum(jnp.sqrt(sq_norm), bound)
    scaled = (out_grads.astype(jnp.float32) * clip_factor[:, None, None]).astype(jnp.bfloat16)
    act_groups = acts.reshape(N_DP, EX_DEV * SEQ, F)
    grad_groups = scaled.reshape(N_DP, EX_DEV * SEQ, D)

    def add_group(total, pair):
        left, right = pair
        partial_sum = lax.dot_general(right, left, (((0,), (0,)), ((), ())), preferred_element_type=jnp.float32)
        return (total + partial_sum, None)
    total, unused = lax.scan(add_group, jnp.zeros((D, F), jnp.float32), (act_groups, grad_groups))
    return (total / EXAMPLES, clip_factor)
```

```python
import functools
import math

import jax
import jax.numpy as jnp
from jax import lax
from jax.experimental import pallas as pl
from jax.experimental.pallas import tpu as pltpu
from jax.sharding import PartitionSpec as P

D = 2304
F = 18432
SEQ = 256
MESH = pl.DeviceIdType.MESH
NZ = 8
SIDE = 4
OWN = 72
EX = 4
TOK = EX * SEQ
COLS = F // NZ
BOUND = math.sqrt(F * D * SEQ)
PIECES = ((0, 32, 1280), (32, 24, 1024), (56, 16, 1280))
TILE = 256
F32, BF16 = jnp.float32, jnp.bfloat16


def tn_dot(a, b):
    return lax.dot_general(a, b, (((0,), (0,)), ((), ())), preferred_element_type=F32)


def nt_dot(a, b):
    return lax.dot_general(a, b, (((1,), (1,)), ((), ())), preferred_element_type=F32)


def kernel(x_hbm, g_hbm, out, clip_out, *scratch):
    names = iter(scratch)
    acts, graw, gt, clipv, tile, parts, agram, ggram = (next(names) for _ in range(8))
    grads = [next(names) for _ in PIECES]
    peer = [next(names) for _ in PIECES]
    scaled = [next(names) for _ in PIECES]
    part = [next(names) for _ in PIECES]
    send1 = [(next(names), next(names)) for _ in PIECES]
    recv1 = [(next(names), next(names)) for _ in PIECES]
    sums = [(next(names), next(names)) for _ in PIECES]
    recv2 = [(next(names), next(names)) for _ in PIECES]
    local_sem, pair_s, pair_r, ring_s, ring_r, norm_s, norm_r, p1_s, p1_r, p2_s, p2_r = names

    dp, z = lax.axis_index("dp"), lax.axis_index("mp")
    y, x, c = dp // 8, (dp // 2) % SIDE, dp % 2
    other = 1 - c

    def at(y, x, c, z):
        return (y * 8 + x * 2 + c, z)

    def xs(k):
        return lax.rem(x + k, SIDE)

    def ys(k):
        return lax.rem(y + k, SIDE)

    def zs(k):
        return lax.rem(z + k + NZ, NZ)

    peer_id = at(y, x, other, z)
    group = [(dz, dc) for dz in range(NZ) for dc in range(2) if dz or dc]

    def group_id(dz, dc):
        return at(y, x, lax.rem(c + dc, 2), zs(dz))

    load_x = pltpu.make_async_copy(x_hbm, acts.at[pl.ds(c * EX, EX)], local_sem.at[0])
    load_g = pltpu.make_async_copy(g_hbm, graw, local_sem.at[1])
    load_g.start()
    load_x.start()

    barrier = pltpu.get_barrier_semaphore()
    for dz, dc in group:
        pl.semaphore_signal(barrier, inc=1, device_id=group_id(dz, dc), device_id_type=MESH)
    for k in range(1, SIDE):
        pl.semaphore_signal(barrier, inc=1, device_id=at(y, xs(k), c, z), device_id_type=MESH)
        pl.semaphore_signal(barrier, inc=1, device_id=at(ys(k), x, c, z), device_id_type=MESH)
    pl.semaphore_wait(barrier, len(group) + 2 * (SIDE - 1))

    def remote(src, dst, ssem, rsem, to):
        return pltpu.make_async_remote_copy(
            src_ref=src, dst_ref=dst, send_sem=ssem, recv_sem=rsem, device_id=to, device_id_type=MESH
        )

    def pair_x():
        here = acts.at[pl.ds(c * EX, EX)]
        return remote(x_hbm, here, pair_s.at[0], pair_r.at[0], peer_id)

    pair_x().start()

    load_g.wait()
    for e in range(EX):
        gt[:, e * SEQ:(e + 1) * SEQ] = graw[e].astype(F32).T
    token0 = pl.multiple_of(c * TOK, TOK)
    token1 = pl.multiple_of(other * TOK, TOK)

    def rows_of(core, first, n):
        return jnp.concatenate(
            [gt[pl.ds(pl.multiple_of(a * 2 * OWN + core * OWN + first, 8), n), :] for a in range(2)], axis=0
        ).astype(BF16)

    def pair_g(p):
        return remote(peer[p], grads[p].at[z, :, pl.ds(token0, TOK)], pair_s.at[1 + p], pair_r.at[1 + p], peer_id)

    for p, (first, n, _) in enumerate(PIECES):
        peer[p][...] = rows_of(other, first, n)
        pair_g(p).start()
        grads[p][z, :, pl.ds(token0, TOK)] = rows_of(c, first, n)

    def ring(p, s, h, q):
        src = zs(-(h - 1) if s == 0 else h - 1)
        view = grads[p].at[src, :, pl.ds(token0 if q == 0 else token1, TOK)]
        return remote(view, view, ring_s.at[p, s, h - 1, q], ring_r.at[p, s, h - 1, q],
                      at(y, x, c, zs(1 if s == 0 else -1)))

    def ring_in(p, s, h, q):
        src = zs(-h if s == 0 else h)
        view = grads[p].at[src, :, pl.ds(token0 if q == 0 else token1, TOK)]
        return remote(view, view, ring_s.at[p, s, h - 1, q], ring_r.at[p, s, h - 1, q],
                      at(y, x, c, zs(1 if s == 0 else -1)))

    def wait_pair_g(p):
        view = grads[p].at[z, :, pl.ds(token1, TOK)]
        remote(peer[p], view, pair_s.at[1 + p], pair_r.at[1 + p], peer_id).wait_recv()

    def ring_step(p, h):
        for q in range(2):
            if h == 1 and q == 1:
                wait_pair_g(p)
            for s in range(2):
                if h == 4 and s != q:
                    continue
                if h > 1:
                    ring_in(p, s, h - 1, q).wait_recv()
                ring(p, s, h, q).start()
        if h == 4:
            for s in range(2):
                ring_in(p, s, 3, 1 - s).wait_recv()

    def ring_last(p):
        for s in range(2):
            ring_in(p, s, 4, s).wait_recv()

    def act_gram(b):
        agram[b] = nt_dot(acts[b], acts[b])

    def grad_gram(p):
        n = PIECES[p][1]

        def body(b, _):
            cols = pl.ds(pl.multiple_of(b * SEQ, SEQ), SEQ)
            v = grads[p][:, :, cols].reshape(NZ * 2 * n, SEQ)
            g = tn_dot(v, v)
            ggram[b] = g if p == 0 else ggram[b] + g
            return 0

        lax.fori_loop(0, 2 * EX, body, 0)

    NP = len(PIECES)
    for p in range(NP):
        for h in range(1, 5):
            ring_step(p, h)
            if p == 0 and h == 2:
                load_x.wait()
                remote(x_hbm, acts.at[pl.ds(other * EX, EX)], pair_s.at[0], pair_r.at[0], peer_id).wait_recv()
            if p == 0 and h >= 3 or p == 1:
                i = (p * 4 + h - 3)
                if i < 4:
                    act_gram(2 * i)
                    act_gram(2 * i + 1)
            if p and h == 1:
                ring_last(p - 1)
                grad_gram(p - 1)
    ring_last(NP - 1)
    grad_gram(NP - 1)

    for b in range(2 * EX):
        v = jnp.sum(agram[b] * ggram[b], axis=0, keepdims=True)
        tile[b:b + 1, :] = v[:, :128] + v[:, 128:]
    slot = z * 2 + c
    parts[slot] = tile[...]

    def norm(i):
        dz, dc = group[i]
        return remote(tile, parts.at[slot], norm_s.at[i], norm_r.at[i], group_id(dz, dc))

    def norm_in(i):
        dz, dc = group[i]
        src = lax.rem(z - dz + NZ, NZ) * 2 + lax.rem(c + dc, 2)
        return remote(tile, parts.at[src], norm_s.at[i], norm_r.at[i], group_id(dz, dc))

    for i in range(len(group)):
        norm(i).start()
    for i in range(len(group)):
        norm_in(i).wait_recv()
    total = jnp.sum(jnp.sum(parts[...], axis=0), axis=1, keepdims=True)
    factor = BOUND / jnp.maximum(jnp.sqrt(total), BOUND)
    for b in range(2 * EX):
        clipv[:, b * SEQ:(b + 1) * SEQ] = jnp.broadcast_to(factor[b:b + 1, :], (1, SEQ))
    for e in range(EX):
        v = clipv[:, pl.ds(pl.multiple_of((c * EX + e) * SEQ, SEQ), 128)]
        clip_out[e] = jnp.max(v)

    def p1(p, half, k):
        to = at(y, xs(k), c, z) if half == 0 else at(ys(k), x, c, z)
        return remote(send1[p][half].at[k - 1], recv1[p][half].at[k - 1],
                      p1_s.at[p, half, k - 1], p1_r.at[p, half, k - 1], to)

    def p2(p, half, k):
        to = at(ys(k), x, c, z) if half == 0 else at(y, xs(k), c, z)
        block = ys(k) if half == 0 else xs(k)
        return remote(sums[p][half].at[block], recv2[p][half].at[k - 1],
                      p2_s.at[p, half, k - 1], p2_r.at[p, half, k - 1], to)

    def span(p, half):
        cut = PIECES[p][2]
        return (0, cut) if half == 0 else (cut, COLS - cut)

    def dests(half, k):
        if half == 0:
            return [i * SIDE + xs(k) for i in range(SIDE)]
        return [ys(k) * SIDE + i for i in range(SIDE)]

    def multiply(p):
        first, n, _ = PIECES[p]
        for zz in range(NZ):
            scaled[p][zz] = (grads[p][zz].astype(F32) * clipv[...]).astype(BF16)
        for half in range(2):
            base, width = span(p, half)

            def body(i, _):
                cols = pl.ds(pl.multiple_of(base + i * TILE, TILE), TILE)
                local = pl.ds(pl.multiple_of(i * TILE, TILE), TILE)
                lhs = scaled[p][...].reshape(NZ * 2 * n, 2 * TOK)
                rhs = acts[:, :, cols].reshape(2 * TOK, TILE)
                part[p][:, :, cols] = jnp.dot(lhs, rhs, preferred_element_type=F32).reshape(16, n, TILE)
                for k in range(1, SIDE):
                    v = jnp.concatenate([part[p][j, :, cols] for j in dests(half, k)], axis=0)
                    send1[p][half][k - 1, :, local] = v.astype(BF16)
                return 0

            lax.fori_loop(0, width // TILE, body, 0)
            for k in range(1, SIDE):
                p1(p, half, k).start()

    def reduce1(p, half):
        first, n, _ = PIECES[p]
        base, width = span(p, half)
        for k in range(1, SIDE):
            p1(p, half, k).wait_recv()

        def body(i, _):
            cols = pl.ds(pl.multiple_of(base + i * TILE, TILE), TILE)
            local = pl.ds(pl.multiple_of(i * TILE, TILE), TILE)
            v = jnp.concatenate([part[p][j, :, cols] for j in dests(half, 0)], axis=0)
            for k in range(1, SIDE):
                v = v + recv1[p][half][k - 1, :, local].astype(F32)
            for i in range(SIDE):
                sums[p][half][i, :, local] = v[i * n:(i + 1) * n]
            return 0

        lax.fori_loop(0, width // TILE, body, 0)
        for k in range(1, SIDE):
            p2(p, half, k).start()

    def reduce2(p, half):
        first, n, _ = PIECES[p]
        base, width = span(p, half)
        for k in range(1, SIDE):
            p2(p, half, k).wait_recv()
        v = sums[p][half][y if half == 0 else x]
        for k in range(1, SIDE):
            v = v + recv2[p][half][k - 1]
        out[first:first + n, base:base + width] = v * (1.0 / 128)

    for p in range(NP):
        multiply(p)
        if p:
            for half in range(2):
                reduce1(p - 1, half)
    for half in range(2):
        reduce1(NP - 1, half)
    for p in range(NP):
        for half in range(2):
            reduce2(p, half)

    pair_x().wait_send()
    for p in range(NP):
        pair_g(p).wait_send()
        for s in range(2):
            for h in range(1, 5):
                for q in range(2):
                    if h < 4 or s == q:
                        ring(p, s, h, q).wait_send()
        for half in range(2):
            for k in range(1, SIDE):
                p1(p, half, k).wait_send()
                p2(p, half, k).wait_send()
    for i in range(len(group)):
        norm(i).wait_send()


def on_device(acts, out_grads):
    np_ = len(PIECES)
    dma = pltpu.SemaphoreType.DMA
    scratch = [
        pltpu.VMEM((2 * EX, SEQ, COLS), BF16),
        pltpu.VMEM((EX, SEQ, D // NZ), BF16),
        pltpu.VMEM((D // NZ, TOK), F32),
        pltpu.VMEM((1, 2 * TOK), F32),
        pltpu.VMEM((2 * EX, 128), F32),
        pltpu.VMEM((2 * NZ, 2 * EX, 128), F32),
        pltpu.VMEM((2 * EX, SEQ, SEQ), F32),
        pltpu.VMEM((2 * EX, SEQ, SEQ), F32),
    ]
    widths = [((0, cut), (1, COLS - cut)) for _, _, cut in PIECES]
    scratch += [pltpu.VMEM((NZ, 2 * n, 2 * TOK), BF16) for _, n, _ in PIECES]
    scratch += [pltpu.VMEM((2 * n, TOK), BF16) for _, n, _ in PIECES]
    scratch += [pltpu.VMEM((NZ, 2 * n, 2 * TOK), BF16) for _, n, _ in PIECES]
    scratch += [pltpu.VMEM((16, n, COLS), F32) for _, n, _ in PIECES]
    for shape in ("send", "recv"):
        scratch += [
            pltpu.VMEM((3, 4 * n, w), BF16) for (_, n, cut) in PIECES for w in (cut, COLS - cut)
        ]
    scratch += [pltpu.VMEM((4, n, w), F32) for (_, n, cut) in PIECES for w in (cut, COLS - cut)]
    scratch += [pltpu.VMEM((3, n, w), F32) for (_, n, cut) in PIECES for w in (cut, COLS - cut)]
    scratch += [
        dma((2,)),
        dma((1 + np_,)),
        dma((1 + np_,)),
        dma((np_, 2, 4, 2)),
        dma((np_, 2, 4, 2)),
        dma((15,)),
        dma((15,)),
        dma((np_, 2, 3)),
        dma((np_, 2, 3)),
        dma((np_, 2, 3)),
        dma((np_, 2, 3)),
    ]
    return pl.pallas_call(
        kernel,
        out_shape=(
            jax.ShapeDtypeStruct((OWN, COLS), F32),
            jax.ShapeDtypeStruct((EX,), F32),
        ),
        in_specs=[pl.BlockSpec(memory_space=pl.ANY)] * 2,
        out_specs=(pl.BlockSpec(memory_space=pltpu.VMEM), pl.BlockSpec(memory_space=pltpu.SMEM)),
        scratch_shapes=scratch,
        compiler_params=pltpu.CompilerParams(
            collective_id=0, has_side_effects=True, vmem_limit_bytes=60 * 2**20
        ),
        name="clipped_grad",
    )(acts, out_grads)


def solution(mesh):
    in_specs = (P("dp", None, "mp"), P("dp", None, "mp"))
    out_specs = (P("dp", "mp"), P("dp"))
    return jax.shard_map(
        on_device, mesh=mesh, in_specs=in_specs, out_specs=out_specs, check_vma=False
    )
```

```python
import functools
import math

import jax
import jax.numpy as jnp
from jax import lax
from jax.experimental import pallas as pl
from jax.experimental.pallas import tpu as pltpu
from jax.sharding import PartitionSpec as P

D = 2304
F = 18432
SEQ = 256
MESH = pl.DeviceIdType.MESH
NZ = 8
SIDE = 4
OWN = 72
EX = 4
TOK = EX * SEQ
COLS = F // NZ
BOUND = math.sqrt(F * D * SEQ)
PIECES = ((0, 16, 1280), (16, 16, 1024), (32, 16, 1280), (48, 16, 1024), (64, 8, 1280))
TILE = 256
ORDER = (
    "g10 g21 a010 g20", "a011 x g31 a020", "g30 a021 g41 a030", "g40 a031 a040 a110", "G a041 a111 a210",
    "a120 n a211 l0", "X s0 m0002 a121", "m0024 a130 m0045 m0102", "a220 m0124 a131 a140", "a221 a141 a230 a310",
    "l1 s1 m1002 a231", "r00 a311 r01 m1024", "a240 m1102 a241 a320", "m1124 a321 m1145 a410", "l2 s2 a411 m2002",
    "a330 m2024 a331 m2045", "a420 m2102 a421 r10", "a340 m2124 a341 R00", "a430 R01 a431 r11", "l3 s3 m3002 a440",
    "a441 m3024 r20 m3102", "m3124 m3145 l4 s4", "r21 m4002 m4024 m4045", "m4102 m4124 R10 r30", "R11 R20 R21 r31",
    "r40 r41 R30 R31", "R40 R41",
)
F32, BF16 = jnp.float32, jnp.bfloat16


def nt_dot(a, b):
    return lax.dot_general(a, b, (((1,), (1,)), ((), ())), preferred_element_type=F32)


def kernel(x_hbm, g_hbm, out, clip_out, *scratch):
    NP = len(PIECES)
    names = iter(scratch)
    acts, graw, gt, clipv, tile, parts, gram, gram_s, gram_r = (next(names) for _ in range(9))
    grads = [next(names) for _ in PIECES]
    peer = [next(names) for _ in PIECES]
    scaled = [next(names) for _ in PIECES]
    part = [next(names) for _ in PIECES]
    send1 = [(next(names), next(names)) for _ in PIECES]
    recv1 = [(next(names), next(names)) for _ in PIECES]
    sums = [(next(names), next(names)) for _ in PIECES]
    recv2 = [(next(names), next(names)) for _ in PIECES]
    far_s = [(next(names), next(names)) for _ in PIECES]
    far_r = [(next(names), next(names)) for _ in PIECES]
    local_sem, gs_s, gs_r, pair_s, pair_r, ring_s, ring_r, norm_s, norm_r, p1_s, p1_r, p2_s, p2_r = names

    dp, z = lax.axis_index("dp"), lax.axis_index("mp")
    y, x, c = dp // 8, (dp // 2) % SIDE, dp % 2
    other = 1 - c

    def at(y, x, c, z):
        return (y * 8 + x * 2 + c, z)

    def xs(k):
        return lax.rem(x + k, SIDE)

    def ys(k):
        return lax.rem(y + k, SIDE)

    def zs(k):
        return lax.rem(z + k + NZ, NZ)

    peer_id = at(y, x, other, z)
    group = [(dz, dc) for dz in range(NZ) for dc in range(2) if dz or dc]

    def group_id(dz, dc):
        return at(y, x, lax.rem(c + dc, 2), zs(dz))

    load_x = pltpu.make_async_copy(x_hbm, acts.at[pl.ds(c * EX, EX)], local_sem.at[0])
    load_g = pltpu.make_async_copy(g_hbm, graw, local_sem.at[1])
    load_g.start()
    load_x.start()

    barrier = pltpu.get_barrier_semaphore()
    for dz, dc in group:
        pl.semaphore_signal(barrier, inc=1, device_id=group_id(dz, dc), device_id_type=MESH)
    for k in range(1, SIDE):
        pl.semaphore_signal(barrier, inc=1, device_id=at(y, xs(k), c, z), device_id_type=MESH)
        pl.semaphore_signal(barrier, inc=1, device_id=at(ys(k), x, c, z), device_id_type=MESH)

    def remote(src, dst, ssem, rsem, to):
        return pltpu.make_async_remote_copy(
            src_ref=src, dst_ref=dst, send_sem=ssem, recv_sem=rsem, device_id=to, device_id_type=MESH
        )

    begun, arrived = [], set()

    def start(copy, *key):
        copy(*key).start()
        begun.append((copy, key))

    def arrive(copy, *key):
        if (copy, key) not in arrived:
            arrived.add((copy, key))
            incoming.get(copy, copy)(*key).wait_recv()

    def pair_x():
        here = acts.at[pl.ds(c * EX, EX)]
        return remote(here, here, pair_s.at[0], pair_r.at[0], peer_id)


    token0 = pl.multiple_of(c * TOK, TOK)
    token1 = pl.multiple_of(other * TOK, TOK)

    def rows_of(core, first, n):
        return jnp.concatenate(
            [gt[pl.ds(pl.multiple_of(a * 2 * OWN + core * OWN + first, 8), n), :] for a in range(2)], axis=0
        ).astype(BF16)

    def pair_g(p):
        return remote(peer[p], grads[p].at[z, :, pl.ds(token0, TOK)], pair_s.at[1 + p], pair_r.at[1 + p], peer_id)

    def ring(p, s, h, q):
        src = zs(-(h - 1) if s == 0 else h - 1)
        view = grads[p].at[src, :, pl.ds(token0 if q == 0 else token1, TOK)]
        return remote(view, view, ring_s.at[p, s, h - 1, q], ring_r.at[p, s, h - 1, q],
                      at(y, x, c, zs(1 if s == 0 else -1)))

    def ring_in(p, s, h, q):
        src = zs(-h if s == 0 else h)
        view = grads[p].at[src, :, pl.ds(token0 if q == 0 else token1, TOK)]
        return remote(view, view, ring_s.at[p, s, h - 1, q], ring_r.at[p, s, h - 1, q],
                      at(y, x, c, zs(1 if s == 0 else -1)))

    def pair_g_in(p):
        view = grads[p].at[z, :, pl.ds(token1, TOK)]
        return remote(peer[p], view, pair_s.at[1 + p], pair_r.at[1 + p], peer_id)

    def ring_step(p, h, q):
        if h == 1 and q == 1:
            arrive(pair_g, p)
        for s in range(2):
            if h == 4 and s != q:
                arrive(ring, p, s, 3, q)
                continue
            if h > 1:
                arrive(ring, p, s, h - 1, q)
            start(ring, p, s, h, q)

    def ring_last(p):
        for s in range(2):
            arrive(ring, p, s, 4, s)

    def local_gram(e):
        for m, v in ((0, acts[c * EX + e]), (1, graw[e])):
            g = nt_dot(v, v)
            for d in range(NZ):
                side = 128 * (d // 4)
                gram[d, 2 * e + m, :32] = g[32 * d:32 * d + 32, side:side + 128]
                gram[d, 2 * e + m, 32:] = g[16 * d:16 * d + 16, 128:]

    def gram_copy(s, h, late):
        part = pl.ds((s ^ late) * EX, EX)
        return remote(gram_s.at[s, h - 1, part], gram_r.at[s, h - 1, part], gs_s.at[s, h - 1, late],
                      gs_r.at[s, h - 1, late], at(y, x, c, zs(1 if s == 0 else -1)))

    def gram_step(h, late):
        for s in range(2):
            d = zs(5 - h if s == 0 else h - 5)
            part = slice((s ^ late) * EX, ((s ^ late) + 1) * EX)
            v = gram[d, part]
            if h > 1 + late:
                arrive(gram_copy, s, h - 1, late)
                v = v + gram_r[s, h - 2, part].astype(F32)
            gram_s[s, h - 1, part] = v.astype(BF16)
            start(gram_copy, s, h, late)

    slot = z * 2 + c

    def gram_last():
        for s in range(2):
            arrive(gram_copy, s, 4, 1)
            arrive(gram_copy, s, 4, 0)
        v = gram[z] + gram_r[0, 3].astype(F32) + gram_r[1, 3].astype(F32)
        v = v.reshape(EX, 2, 48, 128)
        w = v[:, 0] * v[:, 1]
        tile[...] = jnp.sum(w[:, :32], axis=1) + 2.0 * jnp.sum(w[:, 32:], axis=1)
        parts[slot] = tile[...]
        for i in range(len(group)):
            start(norm, i)

    def norm(i):
        dz, dc = group[i]
        return remote(tile, parts.at[slot], norm_s.at[i], norm_r.at[i], group_id(dz, dc))

    def norm_in(i):
        dz, dc = group[i]
        src = lax.rem(z - dz + NZ, NZ) * 2 + lax.rem(c + dc, 2)
        return remote(tile, parts.at[src], norm_s.at[i], norm_r.at[i], group_id(dz, dc))

    def norm_wait():
        for i in range(len(group)):
            arrive(norm, i)
        for core in range(2):
            total = parts[core]
            for zz in range(1, NZ):
                total = total + parts[2 * zz + core]
            total = jnp.sum(total, axis=1, keepdims=True)
            factor = BOUND / jnp.maximum(jnp.sqrt(total), BOUND)
            for e in range(EX):
                b = core * EX + e
                clipv[:, b * SEQ:(b + 1) * SEQ] = jnp.broadcast_to(factor[e:e + 1, :], (1, SEQ))
        for e in range(EX):
            v = clipv[:, pl.ds(pl.multiple_of((c * EX + e) * SEQ, SEQ), 128)]
            clip_out[e] = jnp.max(v)

    def p1(p, half, k):
        to = at(y, xs(k), c, z) if half == 0 else at(ys(k), x, c, z)
        return remote(send1[p][half].at[k - 1], recv1[p][half].at[k - 1],
                      p1_s.at[p, half, k - 1], p1_r.at[p, half, k - 1], to)

    def p2(p, half, k):
        to = at(ys(k), x, c, z) if half == 0 else at(y, xs(k), c, z)
        block = ys(k) if half == 0 else xs(k)
        src, dst = (far_s[p][half], far_r[p][half]) if k == 2 else (sums[p][half].at[block], recv2[p][half].at[k // 2])
        return remote(src, dst, p2_s.at[p, half, k - 1], p2_r.at[p, half, k - 1], to)

    def span(p, half):
        cut = PIECES[p][2]
        return (0, cut) if half == 0 else (cut, COLS - cut)

    def dests(half, k):
        if half == 0:
            return [i * SIDE + xs(k) for i in range(SIDE)]
        return [ys(k) * SIDE + i for i in range(SIDE)]

    def scale(p):
        for zz in range(NZ):
            scaled[p][zz] = (grads[p][zz].astype(F32) * clipv[...]).astype(BF16)

    def multiply(p, half, lo, hi):
        first, n, _ = PIECES[p]
        base, width = span(p, half)

        def body(i, _):
            cols = pl.ds(pl.multiple_of(base + i * TILE, TILE), TILE)
            local = pl.ds(pl.multiple_of(i * TILE, TILE), TILE)
            lhs = scaled[p][...].reshape(NZ * 2 * n, 2 * TOK)
            rhs = acts[:, :, cols].reshape(2 * TOK, TILE)
            part[p][:, :, cols] = jnp.dot(lhs, rhs, preferred_element_type=F32).reshape(16, n, TILE)
            for k in range(1, SIDE):
                v = jnp.concatenate([part[p][j, :, cols] for j in dests(half, k)], axis=0)
                send1[p][half][k - 1, :, local] = v.astype(BF16)
            return 0

        lax.fori_loop(lo, min(hi, width // TILE), body, 0)
        if hi >= width // TILE:
            for k in range(1, SIDE):
                start(p1, p, half, k)

    def reduce1(p, half):
        first, n, _ = PIECES[p]
        base, width = span(p, half)
        for k in range(1, SIDE):
            arrive(p1, p, half, k)

        def body(i, _):
            cols = pl.ds(pl.multiple_of(base + i * TILE, TILE), TILE)
            local = pl.ds(pl.multiple_of(i * TILE, TILE), TILE)
            v = jnp.concatenate([part[p][j, :, cols] for j in dests(half, 0)], axis=0)
            for k in range(1, SIDE):
                v = v + recv1[p][half][k - 1, :, local].astype(F32)
            for i in range(SIDE):
                sums[p][half][i, :, local] = v[i * n:(i + 1) * n]
            return 0

        lax.fori_loop(0, width // TILE, body, 0)
        for k in (1, 3):
            start(p2, p, half, k)
        v = sums[p][half][ys(2) if half == 0 else xs(2)]
        far_s[p][half][...] = jnp.concatenate([v[:, :width // 2], v[:, width // 2:]], axis=0).astype(BF16)
        start(p2, p, half, 2)

    def reduce2(p, half):
        first, n, _ = PIECES[p]
        base, width = span(p, half)
        for k in range(1, SIDE):
            arrive(p2, p, half, k)
        v = sums[p][half][y if half == 0 else x] + recv2[p][half][0] + recv2[p][half][1]
        far = far_r[p][half][...].astype(F32)
        v = v + jnp.concatenate([far[:n], far[n:]], axis=1)
        out[first:first + n, base:base + width] = v * (1.0 / 128)

    def pair_x_in():
        return remote(x_hbm, acts.at[pl.ds(other * EX, EX)], pair_s.at[0], pair_r.at[0], peer_id)

    def wait_pair_x():
        arrive(pair_x)

    def begin_pair_x():
        start(pair_x)

    incoming = {pair_x: pair_x_in, pair_g: pair_g_in, ring: ring_in, norm: norm_in}

    load_g.wait()
    for e in range(EX):
        gt[:, e * SEQ:(e + 1) * SEQ] = graw[e].astype(F32).T
    for p, (first, n, _) in enumerate(PIECES):
        peer[p][...] = rows_of(other, first, n)
        grads[p][z, :, pl.ds(token0, TOK)] = rows_of(c, first, n)

    load_x.wait()
    for e in range(EX):
        local_gram(e)
    pl.semaphore_wait(barrier, len(group) + 2 * (SIDE - 1))
    for p in range(NP):
        start(pair_g, p)

    steps = {
        "a": ring_step,
        "l": ring_last,
        "g": gram_step,
        "G": gram_last,
        "n": norm_wait,
        "x": begin_pair_x,
        "X": wait_pair_x,
        "s": scale,
        "m": multiply,
        "r": reduce1,
        "R": reduce2,
    }
    for word in " ".join(ORDER).split():
        steps[word[0]](*(int(v) for v in word[1:]))

    for copy, key in begun:
        arrive(copy, *key)
        copy(*key).wait_send()


def on_device(acts, out_grads):
    np_ = len(PIECES)
    dma = pltpu.SemaphoreType.DMA
    scratch = [
        pltpu.VMEM((2 * EX, SEQ, COLS), BF16),
        pltpu.VMEM((EX, SEQ, D // NZ), BF16),
        pltpu.VMEM((D // NZ, TOK), F32),
        pltpu.VMEM((1, 2 * TOK), F32),
        pltpu.VMEM((EX, 128), F32),
        pltpu.VMEM((2 * NZ, EX, 128), F32),
        pltpu.VMEM((NZ, 2 * EX, 48, 128), F32),
        pltpu.VMEM((2, 4, 2 * EX, 48, 128), BF16),
        pltpu.VMEM((2, 4, 2 * EX, 48, 128), BF16),
    ]
    widths = [((0, cut), (1, COLS - cut)) for _, _, cut in PIECES]
    scratch += [pltpu.VMEM((NZ, 2 * n, 2 * TOK), BF16) for _, n, _ in PIECES]
    scratch += [pltpu.VMEM((2 * n, TOK), BF16) for _, n, _ in PIECES]
    scratch += [pltpu.VMEM((NZ, 2 * n, 2 * TOK), BF16) for _, n, _ in PIECES]
    scratch += [pltpu.VMEM((16, n, COLS), F32) for _, n, _ in PIECES]
    for shape in ("send", "recv"):
        scratch += [
            pltpu.VMEM((3, 4 * n, w), BF16) for (_, n, cut) in PIECES for w in (cut, COLS - cut)
        ]
    scratch += [pltpu.VMEM((4, n, w), F32) for (_, n, cut) in PIECES for w in (cut, COLS - cut)]
    scratch += [pltpu.VMEM((2, n, w), F32) for (_, n, cut) in PIECES for w in (cut, COLS - cut)]
    for shape in ("send", "recv"):
        scratch += [pltpu.VMEM((2 * n, w // 2), BF16) for (_, n, cut) in PIECES for w in (cut, COLS - cut)]
    scratch += [
        dma((2,)),
        dma((2, 4, 2)),
        dma((2, 4, 2)),
        dma((1 + np_,)),
        dma((1 + np_,)),
        dma((np_, 2, 4, 2)),
        dma((np_, 2, 4, 2)),
        dma((15,)),
        dma((15,)),
        dma((np_, 2, 3)),
        dma((np_, 2, 3)),
        dma((np_, 2, 3)),
        dma((np_, 2, 3)),
    ]
    return pl.pallas_call(
        kernel,
        out_shape=(
            jax.ShapeDtypeStruct((OWN, COLS), F32),
            jax.ShapeDtypeStruct((EX,), F32),
        ),
        in_specs=[pl.BlockSpec(memory_space=pl.ANY)] * 2,
        out_specs=(pl.BlockSpec(memory_space=pltpu.VMEM), pl.BlockSpec(memory_space=pltpu.SMEM)),
        scratch_shapes=scratch,
        compiler_params=pltpu.CompilerParams(
            collective_id=0, has_side_effects=True, vmem_limit_bytes=60 * 2**20
        ),
        name="clipped_grad",
    )(acts, out_grads)


def solution(mesh):
    in_specs = (P("dp", None, "mp"), P("dp", None, "mp"))
    out_specs = (P("dp", "mp"), P("dp"))
    return jax.shard_map(
        on_device, mesh=mesh, in_specs=in_specs, out_specs=out_specs, check_vma=False
    )
```

```python
import functools
import math

import jax
import jax.numpy as jnp
from jax import lax
from jax.experimental import pallas as pl
from jax.experimental.pallas import tpu as pltpu
from jax.sharding import PartitionSpec as P

D = 2304
F = 18432
SEQ = 256
MESH = pl.DeviceIdType.MESH
NZ = 8
SIDE = 4
OWN = 72
EX = 4
TOK = EX * SEQ
COLS = F // NZ
BOUND = math.sqrt(F * D * SEQ)
PIECES = ((0, 16, 1280), (16, 16, 1024), (32, 16, 1280), (48, 16, 1024), (64, 8, 1280))
TILE = 256
ORDER = (
    "g10 g21 a010 g20", "a011 x g31 a020", "g30 a021 g41 a030", "g40 a031 a040 a110", "G a041 a111 a210",
    "a120 n a211 l0", "X s0 m0002 a121", "m0024 a130 m0045 m0102", "a220 m0124 a131 a140", "a221 a141 a230 a310",
    "l1 s1 m1002 a231", "r00 a311 r01 m1024", "a240 m1102 a241 a320", "m1124 a321 m1145 a410", "l2 s2 a411 m2002",
    "a330 m2024 a331 m2045", "a420 m2102 a421 r10", "a340 m2124 a341 R00", "a430 R01 a431 r11", "l3 s3 m3002 a440",
    "a441 m3024 r20 m3102", "m3124 m3145 l4 s4", "r21 m4002 m4024 m4045", "m4102 m4124 R10 r30", "R11 R20 R21 r31",
    "r40 r41 R30 R31", "R40 R41",
)
F32, BF16 = jnp.float32, jnp.bfloat16


def tn_dot(a, b):
    return lax.dot_general(a, b, (((0,), (0,)), ((), ())), preferred_element_type=F32)


def nt_dot(a, b):
    return lax.dot_general(a, b, (((1,), (1,)), ((), ())), preferred_element_type=F32)


def kernel(x_hbm, g_hbm, out_hbm, clip_out, *scratch):
    NP = len(PIECES)
    names = iter(scratch)
    acts, graw, gt, clipv, tile, parts, gram, gram_s, gram_r = (next(names) for _ in range(9))
    grads = [next(names) for _ in PIECES]
    peer = [next(names) for _ in PIECES]
    scaled = [next(names) for _ in PIECES]
    part = [next(names) for _ in PIECES]
    send1 = [(next(names), next(names)) for _ in PIECES]
    recv1 = [(next(names), next(names)) for _ in PIECES]
    sums = [(next(names), next(names)) for _ in PIECES]
    recv2 = [(next(names), next(names)) for _ in PIECES]
    far_s = [(next(names), next(names)) for _ in PIECES]
    far_r = [(next(names), next(names)) for _ in PIECES]
    out, local_sem, out_sem, gs_s, gs_r, pair_s, pair_r, ring_s, ring_r, norm_s, norm_r, p1_s, p1_r, p2_s, p2_r = names

    dp, z = lax.axis_index("dp"), lax.axis_index("mp")
    y, x, c = dp // 8, (dp // 2) % SIDE, dp % 2
    other = 1 - c

    def at(y, x, c, z):
        return (y * 8 + x * 2 + c, z)

    def xs(k):
        return lax.rem(x + k, SIDE)

    def ys(k):
        return lax.rem(y + k, SIDE)

    def zs(k):
        return lax.rem(z + k + NZ, NZ)

    peer_id = at(y, x, other, z)
    group = [(dz, dc) for dz in range(NZ) for dc in range(2) if dz or dc]

    def group_id(dz, dc):
        return at(y, x, lax.rem(c + dc, 2), zs(dz))

    load_x = pltpu.make_async_copy(x_hbm, acts.at[pl.ds(c * EX, EX)], local_sem.at[0])
    load_g = pltpu.make_async_copy(g_hbm, graw, local_sem.at[1])
    load_g.start()
    load_x.start()

    barrier = pltpu.get_barrier_semaphore()
    for dz, dc in group:
        pl.semaphore_signal(barrier, inc=1, device_id=group_id(dz, dc), device_id_type=MESH)
    for k in range(1, SIDE):
        pl.semaphore_signal(barrier, inc=1, device_id=at(y, xs(k), c, z), device_id_type=MESH)
        pl.semaphore_signal(barrier, inc=1, device_id=at(ys(k), x, c, z), device_id_type=MESH)

    def remote(src, dst, ssem, rsem, to):
        return pltpu.make_async_remote_copy(
            src_ref=src, dst_ref=dst, send_sem=ssem, recv_sem=rsem, device_id=to, device_id_type=MESH
        )

    begun, arrived = [], set()

    def start(copy, *key):
        copy(*key).start()
        begun.append((copy, key))

    def arrive(copy, *key):
        if (copy, key) not in arrived:
            arrived.add((copy, key))
            incoming.get(copy, copy)(*key).wait_recv()

    def pair_x():
        here = acts.at[pl.ds(c * EX, EX)]
        return remote(here, here, pair_s.at[0], pair_r.at[0], peer_id)


    token0 = pl.multiple_of(c * TOK, TOK)
    token1 = pl.multiple_of(other * TOK, TOK)

    def rows_of(core, first, n):
        return jnp.concatenate(
            [gt[pl.ds(pl.multiple_of(a * 2 * OWN + core * OWN + first, 8), n), :] for a in range(2)], axis=0
        ).astype(BF16)

    def pair_g(p):
        return remote(peer[p], grads[p].at[z, :, pl.ds(token0, TOK)], pair_s.at[1 + p], pair_r.at[1 + p], peer_id)

    def ring(p, s, h, q):
        src = zs(-(h - 1) if s == 0 else h - 1)
        view = grads[p].at[src, :, pl.ds(token0 if q == 0 else token1, TOK)]
        return remote(view, view, ring_s.at[p, s, h - 1, q], ring_r.at[p, s, h - 1, q],
                      at(y, x, c, zs(1 if s == 0 else -1)))

    def ring_in(p, s, h, q):
        src = zs(-h if s == 0 else h)
        view = grads[p].at[src, :, pl.ds(token0 if q == 0 else token1, TOK)]
        return remote(view, view, ring_s.at[p, s, h - 1, q], ring_r.at[p, s, h - 1, q],
                      at(y, x, c, zs(1 if s == 0 else -1)))

    def pair_g_in(p):
        view = grads[p].at[z, :, pl.ds(token1, TOK)]
        return remote(peer[p], view, pair_s.at[1 + p], pair_r.at[1 + p], peer_id)

    def ring_step(p, h, q):
        if h == 1 and q == 1:
            arrive(pair_g, p)
        for s in range(2):
            if h == 4 and s != q:
                arrive(ring, p, s, 3, q)
                continue
            if h > 1:
                arrive(ring, p, s, h - 1, q)
            start(ring, p, s, h, q)

    def ring_last(p):
        for s in range(2):
            arrive(ring, p, s, 4, s)

    def local_gram(e):
        v = acts[c * EX + e]
        for m, g in ((0, nt_dot(v, v)), (1, tn_dot(graw[e], graw[e]))):
            for d in range(NZ):
                side = 128 * (d // 4)
                gram[d, 2 * e + m, :32] = g[32 * d:32 * d + 32, side:side + 128]
                gram[d, 2 * e + m, 32:] = g[16 * d:16 * d + 16, 128:]

    def gram_copy(s, h, late):
        part = pl.ds((s ^ late) * EX, EX)
        return remote(gram_s.at[s, h - 1, part], gram_r.at[s, h - 1, part], gs_s.at[s, h - 1, late],
                      gs_r.at[s, h - 1, late], at(y, x, c, zs(1 if s == 0 else -1)))

    def gram_step(h, late):
        for s in range(2):
            d = zs(5 - h if s == 0 else h - 5)
            part = slice((s ^ late) * EX, ((s ^ late) + 1) * EX)
            v = gram[d, part]
            if h > 1 + late:
                arrive(gram_copy, s, h - 1, late)
                v = v + gram_r[s, h - 2, part].astype(F32)
            gram_s[s, h - 1, part] = v.astype(BF16)
            start(gram_copy, s, h, late)

    slot = z * 2 + c

    def gram_last():
        for s in range(2):
            arrive(gram_copy, s, 4, 1)
            arrive(gram_copy, s, 4, 0)
        v = gram[z] + gram_r[0, 3].astype(F32) + gram_r[1, 3].astype(F32)
        v = v.reshape(EX, 2, 48, 128)
        w = v[:, 0] * v[:, 1]
        tile[...] = jnp.sum(w[:, :32], axis=1) + 2.0 * jnp.sum(w[:, 32:], axis=1)
        parts[slot] = tile[...]
        for i in range(len(group)):
            start(norm, i)

    def norm(i):
        dz, dc = group[i]
        return remote(tile, parts.at[slot], norm_s.at[i], norm_r.at[i], group_id(dz, dc))

    def norm_in(i):
        dz, dc = group[i]
        src = lax.rem(z - dz + NZ, NZ) * 2 + lax.rem(c + dc, 2)
        return remote(tile, parts.at[src], norm_s.at[i], norm_r.at[i], group_id(dz, dc))

    def norm_wait():
        for i in range(len(group)):
            arrive(norm, i)
        for core in range(2):
            total = parts[core]
            for zz in range(1, NZ):
                total = total + parts[2 * zz + core]
            total = jnp.sum(total, axis=1, keepdims=True)
            factor = BOUND / jnp.maximum(jnp.sqrt(total), BOUND)
            for e in range(EX):
                b = core * EX + e
                clipv[:, b * SEQ:(b + 1) * SEQ] = jnp.broadcast_to(factor[e:e + 1, :], (1, SEQ))
        for e in range(EX):
            v = clipv[:, pl.ds(pl.multiple_of((c * EX + e) * SEQ, SEQ), 128)]
            clip_out[e] = jnp.max(v)

    def p1(p, half, k):
        to = at(y, xs(k), c, z) if half == 0 else at(ys(k), x, c, z)
        return remote(send1[p][half].at[k - 1], recv1[p][half].at[k - 1],
                      p1_s.at[p, half, k - 1], p1_r.at[p, half, k - 1], to)

    def p2(p, half, k):
        to = at(ys(k), x, c, z) if half == 0 else at(y, xs(k), c, z)
        block = ys(k) if half == 0 else xs(k)
        src, dst = (far_s[p][half], far_r[p][half]) if k == 2 else (sums[p][half].at[block], recv2[p][half].at[k // 2])
        return remote(src, dst, p2_s.at[p, half, k - 1], p2_r.at[p, half, k - 1], to)

    def span(p, half):
        cut = PIECES[p][2]
        return (0, cut) if half == 0 else (cut, COLS - cut)

    def dests(half, k):
        if half == 0:
            return [i * SIDE + xs(k) for i in range(SIDE)]
        return [ys(k) * SIDE + i for i in range(SIDE)]

    def scale(p):
        for zz in range(NZ):
            scaled[p][zz] = (grads[p][zz].astype(F32) * clipv[...]).astype(BF16)

    def multiply(p, half, lo, hi):
        first, n, _ = PIECES[p]
        base, width = span(p, half)

        def body(i, _):
            cols = pl.ds(pl.multiple_of(base + i * TILE, TILE), TILE)
            local = pl.ds(pl.multiple_of(i * TILE, TILE), TILE)
            lhs = scaled[p][...].reshape(NZ * 2 * n, 2 * TOK)
            rhs = acts[:, :, cols].reshape(2 * TOK, TILE)
            part[p][:, :, cols] = jnp.dot(lhs, rhs, preferred_element_type=F32).reshape(16, n, TILE)
            for k in range(1, SIDE):
                v = jnp.concatenate([part[p][j, :, cols] for j in dests(half, k)], axis=0)
                send1[p][half][k - 1, :, local] = v.astype(BF16)
            return 0

        lax.fori_loop(lo, min(hi, width // TILE), body, 0)
        if hi >= width // TILE:
            for k in range(1, SIDE):
                start(p1, p, half, k)

    def reduce1(p, half):
        first, n, _ = PIECES[p]
        base, width = span(p, half)
        for k in range(1, SIDE):
            arrive(p1, p, half, k)

        def body(i, _):
            cols = pl.ds(pl.multiple_of(base + i * TILE, TILE), TILE)
            local = pl.ds(pl.multiple_of(i * TILE, TILE), TILE)
            v = jnp.concatenate([part[p][j, :, cols] for j in dests(half, 0)], axis=0)
            for k in range(1, SIDE):
                v = v + recv1[p][half][k - 1, :, local].astype(F32)
            for i in range(SIDE):
                sums[p][half][i, :, local] = v[i * n:(i + 1) * n]
            return 0

        lax.fori_loop(0, width // TILE, body, 0)
        for k in (1, 3):
            start(p2, p, half, k)
        v = sums[p][half][ys(2) if half == 0 else xs(2)]
        far_s[p][half][...] = jnp.concatenate([v[:, :width // 2], v[:, width // 2:]], axis=0).astype(BF16)
        start(p2, p, half, 2)

    stored = []

    def store(p, half):
        first, n, _ = PIECES[p]
        base, width = span(p, half)
        view = (pl.ds(first, n), pl.ds(base, width))
        return pltpu.make_async_copy(out.at[view], out_hbm.at[view], out_sem.at[p, half])

    def reduce2(p, half):
        first, n, _ = PIECES[p]
        base, width = span(p, half)
        for k in range(1, SIDE):
            arrive(p2, p, half, k)
        v = sums[p][half][y if half == 0 else x] + recv2[p][half][0] + recv2[p][half][1]
        far = far_r[p][half][...].astype(F32)
        v = v + jnp.concatenate([far[:n], far[n:]], axis=1)
        out[first:first + n, base:base + width] = v * (1.0 / 128)
        store(p, half).start()
        stored.append((p, half))

    def pair_x_in():
        return remote(x_hbm, acts.at[pl.ds(other * EX, EX)], pair_s.at[0], pair_r.at[0], peer_id)

    def wait_pair_x():
        arrive(pair_x)

    def begin_pair_x():
        start(pair_x)

    incoming = {pair_x: pair_x_in, pair_g: pair_g_in, ring: ring_in, norm: norm_in}

    load_g.wait()
    for e in range(EX):
        gt[:, e * SEQ:(e + 1) * SEQ] = graw[e].astype(F32)
    for p, (first, n, _) in enumerate(PIECES):
        peer[p][...] = rows_of(other, first, n)
        grads[p][z, :, pl.ds(token0, TOK)] = rows_of(c, first, n)

    load_x.wait()
    for e in range(EX):
        local_gram(e)
    pl.semaphore_wait(barrier, len(group) + 2 * (SIDE - 1))
    for p in range(NP):
        start(pair_g, p)

    steps = {
        "a": ring_step,
        "l": ring_last,
        "g": gram_step,
        "G": gram_last,
        "n": norm_wait,
        "x": begin_pair_x,
        "X": wait_pair_x,
        "s": scale,
        "m": multiply,
        "r": reduce1,
        "R": reduce2,
    }
    for word in " ".join(ORDER).split():
        steps[word[0]](*(int(v) for v in word[1:]))

    for key in stored:
        store(*key).wait()
    for copy, key in begun:
        arrive(copy, *key)
        copy(*key).wait_send()


def hand_on(total, factor, out, clip_out):
    out[...] = total[...]
    for e in range(EX):
        clip_out[e] = factor[e]


def on_device(acts, out_grads):
    np_ = len(PIECES)
    dma = pltpu.SemaphoreType.DMA
    scratch = [
        pltpu.VMEM((2 * EX, SEQ, COLS), BF16),
        pltpu.VMEM((EX, D // NZ, SEQ), BF16),
        pltpu.VMEM((D // NZ, TOK), F32),
        pltpu.VMEM((1, 2 * TOK), F32),
        pltpu.VMEM((EX, 128), F32),
        pltpu.VMEM((2 * NZ, EX, 128), F32),
        pltpu.VMEM((NZ, 2 * EX, 48, 128), F32),
        pltpu.VMEM((2, 4, 2 * EX, 48, 128), BF16),
        pltpu.VMEM((2, 4, 2 * EX, 48, 128), BF16),
    ]
    widths = [((0, cut), (1, COLS - cut)) for _, _, cut in PIECES]
    scratch += [pltpu.VMEM((NZ, 2 * n, 2 * TOK), BF16) for _, n, _ in PIECES]
    scratch += [pltpu.VMEM((2 * n, TOK), BF16) for _, n, _ in PIECES]
    scratch += [pltpu.VMEM((NZ, 2 * n, 2 * TOK), BF16) for _, n, _ in PIECES]
    scratch += [pltpu.VMEM((16, n, COLS), F32) for _, n, _ in PIECES]
    for shape in ("send", "recv"):
        scratch += [
            pltpu.VMEM((3, 4 * n, w), BF16) for (_, n, cut) in PIECES for w in (cut, COLS - cut)
        ]
    scratch += [pltpu.VMEM((4, n, w), F32) for (_, n, cut) in PIECES for w in (cut, COLS - cut)]
    scratch += [pltpu.VMEM((2, n, w), F32) for (_, n, cut) in PIECES for w in (cut, COLS - cut)]
    for shape in ("send", "recv"):
        scratch += [pltpu.VMEM((2 * n, w // 2), BF16) for (_, n, cut) in PIECES for w in (cut, COLS - cut)]
    scratch += [
        pltpu.VMEM((OWN, COLS), F32),
        dma((2,)),
        dma((np_, 2)),
        dma((2, 4, 2)),
        dma((2, 4, 2)),
        dma((1 + np_,)),
        dma((1 + np_,)),
        dma((np_, 2, 4, 2)),
        dma((np_, 2, 4, 2)),
        dma((15,)),
        dma((15,)),
        dma((np_, 2, 3)),
        dma((np_, 2, 3)),
        dma((np_, 2, 3)),
        dma((np_, 2, 3)),
    ]
    total, factor = pl.pallas_call(
        kernel,
        out_shape=(
            jax.ShapeDtypeStruct((OWN, COLS), F32),
            jax.ShapeDtypeStruct((EX,), F32),
        ),
        in_specs=[pl.BlockSpec(memory_space=pl.ANY)] * 2,
        out_specs=(pl.BlockSpec(memory_space=pl.ANY), pl.BlockSpec(memory_space=pltpu.SMEM)),
        scratch_shapes=scratch,
        compiler_params=pltpu.CompilerParams(
            collective_id=0, has_side_effects=True, vmem_limit_bytes=60 * 2**20
        ),
        name="clipped_grad",
    )(acts, jnp.swapaxes(out_grads, 1, 2))
    return pl.pallas_call(
        hand_on,
        out_shape=(
            jax.ShapeDtypeStruct((OWN, COLS), F32),
            jax.ShapeDtypeStruct((EX,), F32),
        ),
        in_specs=[pl.BlockSpec(memory_space=pltpu.VMEM), pl.BlockSpec(memory_space=pltpu.SMEM)],
        out_specs=(pl.BlockSpec(memory_space=pltpu.VMEM), pl.BlockSpec(memory_space=pltpu.SMEM)),
        name="hand_on",
    )(total, factor)


def solution(mesh):
    in_specs = (P("dp", None, "mp"), P("dp", None, "mp"))
    out_specs = (P("dp", "mp"), P("dp"))
    return jax.shard_map(
        on_device, mesh=mesh, in_specs=in_specs, out_specs=out_specs, check_vma=False
    )
```

```python
import functools
import math

import jax
import jax.numpy as jnp
from jax import lax
from jax.experimental import pallas as pl
from jax.experimental.pallas import tpu as pltpu
from jax.sharding import PartitionSpec as P

D = 2304
F = 18432
SEQ = 256
MESH = pl.DeviceIdType.MESH
NZ = 8
SIDE = 4
OWN = 72
EX = 4
TOK = EX * SEQ
COLS = F // NZ
BOUND = math.sqrt(F * D * SEQ)
PIECES = ((0, 16, 1280), (16, 16, 1024), (32, 16, 1280), (48, 16, 1024), (64, 8, 1280))
TILE = 256
HALF = 160
ORDER = (
    "g10 g21 a010 g20", "a011 x a110 g31", "g30 a020 a021 a111", "g41 g40 a030 a031", "a120 G a040 a041",
    "a121 a130 n a210", "l0 X s0 a211", "m0001 m0012 m0023 a131", "m0034 m0045 a140 m0101", "m0112 a220 m0123 m0134",
    "a141 a221 a310 l1", "s1 m1001 a311 m1012", "m1023 a230 m1034 m1101", "m1112 a231 m1123 r00", "a320 r01 a321 m1134",
    "m1145 a240 a241 a330", "R00 a410 r10 a331", "l2 s2 a411 m2001", "m2012 a340 m2023 m2034", "a420 m2045 m2101 a341",
    "a421 r11 m2112 m2123", "m2134 a430 l3 s3", "m3001 m3012 a431 m3023", "m3034 m3101 m3112 a440", "m3123 m3134 m3145 a441",
    "R01 R10 r20 l4", "s4 m4001 r21 m4012", "m4023 m4034 m4045 m4101", "m4112 m4123 m4134 R11", "r30 r31 R21 R20",
    "r40 r41 R31 R30", "R40 R41",
)
F32, BF16 = jnp.float32, jnp.bfloat16


def tn_dot(a, b):
    return lax.dot_general(a, b, (((0,), (0,)), ((), ())), preferred_element_type=F32)


def nt_dot(a, b):
    return lax.dot_general(a, b, (((1,), (1,)), ((), ())), preferred_element_type=F32)


def kernel(x_hbm, g_hbm, out_hbm, clip_out, *scratch):
    NP = len(PIECES)
    names = iter(scratch)
    acts, graw, gt, clipv, tile, parts, gram, gram_s, gram_r = (next(names) for _ in range(9))
    grads = [next(names) for _ in PIECES]
    peer = [next(names) for _ in PIECES]
    scaled = [next(names) for _ in PIECES]
    part = [next(names) for _ in PIECES]
    send1 = [(next(names), next(names)) for _ in PIECES]
    recv1 = [(next(names), next(names)) for _ in PIECES]
    sums = [(next(names), next(names)) for _ in PIECES]
    recv2 = [(next(names), next(names)) for _ in PIECES]
    far_s = [(next(names), next(names)) for _ in PIECES]
    far_r = [(next(names), next(names)) for _ in PIECES]
    out, local_sem, out_sem, gs_s, gs_r, pair_s, pair_r, ring_s, ring_r, norm_s, norm_r, p1_s, p1_r, p2_s, p2_r = names

    dp, z = lax.axis_index("dp"), lax.axis_index("mp")
    y, x, c = dp // 8, (dp // 2) % SIDE, dp % 2
    other = 1 - c

    def at(y, x, c, z):
        return (y * 8 + x * 2 + c, z)

    def xs(k):
        return lax.rem(x + k, SIDE)

    def ys(k):
        return lax.rem(y + k, SIDE)

    def zs(k):
        return lax.rem(z + k + NZ, NZ)

    peer_id = at(y, x, other, z)
    group = [(dz, dc) for dz in range(NZ) for dc in range(2) if dz or dc]

    def group_id(dz, dc):
        return at(y, x, lax.rem(c + dc, 2), zs(dz))

    load_x = pltpu.make_async_copy(x_hbm, acts.at[pl.ds(c * EX, EX)], local_sem.at[0])
    load_g = pltpu.make_async_copy(g_hbm, graw, local_sem.at[1])
    load_g.start()
    load_x.start()

    barrier = pltpu.get_barrier_semaphore()
    for dz, dc in group:
        pl.semaphore_signal(barrier, inc=1, device_id=group_id(dz, dc), device_id_type=MESH)
    for k in range(1, SIDE):
        pl.semaphore_signal(barrier, inc=1, device_id=at(y, xs(k), c, z), device_id_type=MESH)
        pl.semaphore_signal(barrier, inc=1, device_id=at(ys(k), x, c, z), device_id_type=MESH)

    def remote(src, dst, ssem, rsem, to):
        return pltpu.make_async_remote_copy(
            src_ref=src, dst_ref=dst, send_sem=ssem, recv_sem=rsem, device_id=to, device_id_type=MESH
        )

    begun, arrived = [], set()

    def start(copy, *key):
        copy(*key).start()
        begun.append((copy, key))

    def arrive(copy, *key):
        if (copy, key) not in arrived:
            arrived.add((copy, key))
            incoming.get(copy, copy)(*key).wait_recv()

    def pair_x():
        here = acts.at[pl.ds(c * EX, EX)]
        return remote(here, here, pair_s.at[0], pair_r.at[0], peer_id)


    token0 = pl.multiple_of(c * TOK, TOK)
    token1 = pl.multiple_of(other * TOK, TOK)

    def rows_of(core, first, n):
        return jnp.concatenate(
            [gt[pl.ds(pl.multiple_of(a * 2 * OWN + core * OWN + first, 8), n), :] for a in range(2)], axis=0
        ).astype(BF16)

    def pair_g(p):
        return remote(peer[p], grads[p].at[z, :, pl.ds(token0, TOK)], pair_s.at[1 + p], pair_r.at[1 + p], peer_id)

    def ring(p, s, h, q):
        src = zs(-(h - 1) if s == 0 else h - 1)
        view = grads[p].at[src, :, pl.ds(token0 if q == 0 else token1, TOK)]
        return remote(view, view, ring_s.at[p, s, h - 1, q], ring_r.at[p, s, h - 1, q],
                      at(y, x, c, zs(1 if s == 0 else -1)))

    def ring_in(p, s, h, q):
        src = zs(-h if s == 0 else h)
        view = grads[p].at[src, :, pl.ds(token0 if q == 0 else token1, TOK)]
        return remote(view, view, ring_s.at[p, s, h - 1, q], ring_r.at[p, s, h - 1, q],
                      at(y, x, c, zs(1 if s == 0 else -1)))

    def pair_g_in(p):
        view = grads[p].at[z, :, pl.ds(token1, TOK)]
        return remote(peer[p], view, pair_s.at[1 + p], pair_r.at[1 + p], peer_id)

    def ring_step(p, h, q):
        if h == 1 and q == 1:
            arrive(pair_g, p)
        for s in range(2):
            if h == 4 and s != q:
                arrive(ring, p, s, 3, q)
                continue
            if h > 1:
                arrive(ring, p, s, h - 1, q)
            start(ring, p, s, h, q)

    def ring_last(p):
        for s in range(2):
            arrive(ring, p, s, 4, s)

    def local_gram(e):
        v = acts[c * EX + e]
        for m, g in ((0, nt_dot(v, v)), (1, tn_dot(graw[e], graw[e]))):
            blocks = [g[64 * i:64 * i + 64, 64 * i:64 * i + 128] for i in range(3)]
            blocks.append(jnp.concatenate([g[192:, 192:], g[192:, :64]], axis=1))
            blocks.append(jnp.concatenate([g[:64, 128:192], g[64:128, 192:]], axis=1))
            for i, block in enumerate(blocks):
                row = (2 * e + m) * 40 + 8 * i
                for d in range(NZ):
                    gram[d, row:row + 8] = block[8 * d:8 * d + 8]

    def gram_copy(s, h, late):
        part = pl.ds((s ^ late) * HALF, HALF)
        return remote(gram_s.at[s, h - 1, part], gram_r.at[s, h - 1, part], gs_s.at[s, h - 1, late],
                      gs_r.at[s, h - 1, late], at(y, x, c, zs(1 if s == 0 else -1)))

    def gram_step(h, late):
        for s in range(2):
            d = zs(5 - h if s == 0 else h - 5)
            part = slice((s ^ late) * HALF, ((s ^ late) + 1) * HALF)
            v = gram[d, part]
            if h > 1 + late:
                arrive(gram_copy, s, h - 1, late)
                v = v + gram_r[s, h - 2, part].astype(F32)
            gram_s[s, h - 1, part] = v.astype(BF16)
            start(gram_copy, s, h, late)

    slot = z * 2 + c

    def gram_last():
        for s in range(2):
            arrive(gram_copy, s, 4, 1)
            arrive(gram_copy, s, 4, 0)
        v = gram[z] + gram_r[0, 3].astype(F32) + gram_r[1, 3].astype(F32)
        v = v.reshape(EX, 2, 40, 128)
        w = v[:, 0] * v[:, 1]
        twice = 1.0 + (lax.broadcasted_iota(jnp.int32, (EX, 128), 1) >= 64).astype(F32)
        tile[...] = twice * jnp.sum(w[:, :32], axis=1) + 2.0 * jnp.sum(w[:, 32:], axis=1)
        parts[slot] = tile[...]
        for i in range(len(group)):
            start(norm, i)

    def norm(i):
        dz, dc = group[i]
        return remote(tile, parts.at[slot], norm_s.at[i], norm_r.at[i], group_id(dz, dc))

    def norm_in(i):
        dz, dc = group[i]
        src = lax.rem(z - dz + NZ, NZ) * 2 + lax.rem(c + dc, 2)
        return remote(tile, parts.at[src], norm_s.at[i], norm_r.at[i], group_id(dz, dc))

    def norm_wait():
        for i in range(len(group)):
            arrive(norm, i)
        for core in range(2):
            total = parts[core]
            for zz in range(1, NZ):
                total = total + parts[2 * zz + core]
            total = jnp.sum(total, axis=1, keepdims=True)
            factor = BOUND / jnp.maximum(jnp.sqrt(total), BOUND)
            for e in range(EX):
                b = core * EX + e
                clipv[:, b * SEQ:(b + 1) * SEQ] = jnp.broadcast_to(factor[e:e + 1, :], (1, SEQ))
        for e in range(EX):
            v = clipv[:, pl.ds(pl.multiple_of((c * EX + e) * SEQ, SEQ), 128)]
            clip_out[e] = jnp.max(v)

    def p1(p, half, k):
        to = at(y, xs(k), c, z) if half == 0 else at(ys(k), x, c, z)
        return remote(send1[p][half].at[k - 1], recv1[p][half].at[k - 1],
                      p1_s.at[p, half, k - 1], p1_r.at[p, half, k - 1], to)

    def p2(p, half, k):
        to = at(ys(k), x, c, z) if half == 0 else at(y, xs(k), c, z)
        block = ys(k) if half == 0 else xs(k)
        src, dst = (far_s[p][half], far_r[p][half]) if k == 2 else (sums[p][half].at[block], recv2[p][half].at[k // 2])
        return remote(src, dst, p2_s.at[p, half, k - 1], p2_r.at[p, half, k - 1], to)

    def span(p, half):
        cut = PIECES[p][2]
        return (0, cut) if half == 0 else (cut, COLS - cut)

    def dests(half, k):
        if half == 0:
            return [i * SIDE + xs(k) for i in range(SIDE)]
        return [ys(k) * SIDE + i for i in range(SIDE)]

    def scale(p):
        for zz in range(NZ):
            scaled[p][zz] = (grads[p][zz].astype(F32) * clipv[...]).astype(BF16)

    def multiply(p, half, lo, hi):
        first, n, _ = PIECES[p]
        base, width = span(p, half)

        def body(i, _):
            cols = pl.ds(pl.multiple_of(base + i * TILE, TILE), TILE)
            local = pl.ds(pl.multiple_of(i * TILE, TILE), TILE)
            lhs = scaled[p][...].reshape(NZ * 2 * n, 2 * TOK)
            rhs = acts[:, :, cols].reshape(2 * TOK, TILE)
            part[p][:, :, cols] = jnp.dot(lhs, rhs, preferred_element_type=F32).reshape(16, n, TILE)
            for k in range(1, SIDE):
                v = jnp.concatenate([part[p][j, :, cols] for j in dests(half, k)], axis=0)
                send1[p][half][k - 1, :, local] = v.astype(BF16)
            return 0

        lax.fori_loop(lo, min(hi, width // TILE), body, 0)
        if hi >= width // TILE:
            for k in range(1, SIDE):
                start(p1, p, half, k)

    def reduce1(p, half):
        first, n, _ = PIECES[p]
        base, width = span(p, half)
        for k in range(1, SIDE):
            arrive(p1, p, half, k)

        def body(i, _):
            cols = pl.ds(pl.multiple_of(base + i * TILE, TILE), TILE)
            local = pl.ds(pl.multiple_of(i * TILE, TILE), TILE)
            v = jnp.concatenate([part[p][j, :, cols] for j in dests(half, 0)], axis=0)
            for k in range(1, SIDE):
                v = v + recv1[p][half][k - 1, :, local].astype(F32)
            for i in range(SIDE):
                sums[p][half][i, :, local] = v[i * n:(i + 1) * n]
            return 0

        lax.fori_loop(0, width // TILE, body, 0)
        for k in (1, 3):
            start(p2, p, half, k)
        v = sums[p][half][ys(2) if half == 0 else xs(2)]
        far_s[p][half][...] = jnp.concatenate([v[:, :width // 2], v[:, width // 2:]], axis=0).astype(BF16)
        start(p2, p, half, 2)

    stored = []

    def store(p, half):
        first, n, _ = PIECES[p]
        base, width = span(p, half)
        view = (pl.ds(first, n), pl.ds(base, width))
        return pltpu.make_async_copy(out.at[view], out_hbm.at[view], out_sem.at[p, half])

    def reduce2(p, half):
        first, n, _ = PIECES[p]
        base, width = span(p, half)
        for k in range(1, SIDE):
            arrive(p2, p, half, k)
        v = sums[p][half][y if half == 0 else x] + recv2[p][half][0] + recv2[p][half][1]
        far = far_r[p][half][...].astype(F32)
        v = v + jnp.concatenate([far[:n], far[n:]], axis=1)
        out[first:first + n, base:base + width] = v * (1.0 / 128)
        store(p, half).start()
        stored.append((p, half))

    def pair_x_in():
        return remote(x_hbm, acts.at[pl.ds(other * EX, EX)], pair_s.at[0], pair_r.at[0], peer_id)

    def wait_pair_x():
        arrive(pair_x)

    def begin_pair_x():
        start(pair_x)

    incoming = {pair_x: pair_x_in, pair_g: pair_g_in, ring: ring_in, norm: norm_in}

    load_g.wait()
    for e in range(EX):
        gt[:, e * SEQ:(e + 1) * SEQ] = graw[e].astype(F32)
    for p, (first, n, _) in enumerate(PIECES):
        peer[p][...] = rows_of(other, first, n)
        grads[p][z, :, pl.ds(token0, TOK)] = rows_of(c, first, n)

    load_x.wait()
    for e in range(EX):
        local_gram(e)
    pl.semaphore_wait(barrier, len(group) + 2 * (SIDE - 1))
    for p in range(NP):
        start(pair_g, p)

    steps = {
        "a": ring_step,
        "l": ring_last,
        "g": gram_step,
        "G": gram_last,
        "n": norm_wait,
        "x": begin_pair_x,
        "X": wait_pair_x,
        "s": scale,
        "m": multiply,
        "r": reduce1,
        "R": reduce2,
    }
    for word in " ".join(ORDER).split():
        steps[word[0]](*(int(v) for v in word[1:]))

    for key in stored:
        store(*key).wait()
    for copy, key in begun:
        arrive(copy, *key)
        copy(*key).wait_send()


def hand_on(total, factor, out, clip_out):
    out[...] = total[...]
    for e in range(EX):
        clip_out[e] = factor[e]


def on_device(acts, out_grads):
    np_ = len(PIECES)
    dma = pltpu.SemaphoreType.DMA
    scratch = [
        pltpu.VMEM((2 * EX, SEQ, COLS), BF16),
        pltpu.VMEM((EX, D // NZ, SEQ), BF16),
        pltpu.VMEM((D // NZ, TOK), F32),
        pltpu.VMEM((1, 2 * TOK), F32),
        pltpu.VMEM((EX, 128), F32),
        pltpu.VMEM((2 * NZ, EX, 128), F32),
        pltpu.VMEM((NZ, 2 * HALF, 128), F32),
        pltpu.VMEM((2, 4, 2 * HALF, 128), BF16),
        pltpu.VMEM((2, 4, 2 * HALF, 128), BF16),
    ]
    widths = [((0, cut), (1, COLS - cut)) for _, _, cut in PIECES]
    scratch += [pltpu.VMEM((NZ, 2 * n, 2 * TOK), BF16) for _, n, _ in PIECES]
    scratch += [pltpu.VMEM((2 * n, TOK), BF16) for _, n, _ in PIECES]
    scratch += [pltpu.VMEM((NZ, 2 * n, 2 * TOK), BF16) for _, n, _ in PIECES]
    scratch += [pltpu.VMEM((16, n, COLS), F32) for _, n, _ in PIECES]
    for shape in ("send", "recv"):
        scratch += [
            pltpu.VMEM((3, 4 * n, w), BF16) for (_, n, cut) in PIECES for w in (cut, COLS - cut)
        ]
    scratch += [pltpu.VMEM((4, n, w), F32) for (_, n, cut) in PIECES for w in (cut, COLS - cut)]
    scratch += [pltpu.VMEM((2, n, w), F32) for (_, n, cut) in PIECES for w in (cut, COLS - cut)]
    for shape in ("send", "recv"):
        scratch += [pltpu.VMEM((2 * n, w // 2), BF16) for (_, n, cut) in PIECES for w in (cut, COLS - cut)]
    scratch += [
        pltpu.VMEM((OWN, COLS), F32),
        dma((2,)),
        dma((np_, 2)),
        dma((2, 4, 2)),
        dma((2, 4, 2)),
        dma((1 + np_,)),
        dma((1 + np_,)),
        dma((np_, 2, 4, 2)),
        dma((np_, 2, 4, 2)),
        dma((15,)),
        dma((15,)),
        dma((np_, 2, 3)),
        dma((np_, 2, 3)),
        dma((np_, 2, 3)),
        dma((np_, 2, 3)),
    ]
    total, factor = pl.pallas_call(
        kernel,
        out_shape=(
            jax.ShapeDtypeStruct((OWN, COLS), F32),
            jax.ShapeDtypeStruct((EX,), F32),
        ),
        in_specs=[pl.BlockSpec(memory_space=pl.ANY)] * 2,
        out_specs=(pl.BlockSpec(memory_space=pl.ANY), pl.BlockSpec(memory_space=pltpu.SMEM)),
        scratch_shapes=scratch,
        compiler_params=pltpu.CompilerParams(
            collective_id=0, has_side_effects=True, vmem_limit_bytes=60 * 2**20
        ),
        name="clipped_grad",
    )(acts, jnp.swapaxes(out_grads, 1, 2))
    return pl.pallas_call(
        hand_on,
        out_shape=(
            jax.ShapeDtypeStruct((OWN, COLS), F32),
            jax.ShapeDtypeStruct((EX,), F32),
        ),
        in_specs=[pl.BlockSpec(memory_space=pltpu.VMEM), pl.BlockSpec(memory_space=pltpu.SMEM)],
        out_specs=(pl.BlockSpec(memory_space=pltpu.VMEM), pl.BlockSpec(memory_space=pltpu.SMEM)),
        name="hand_on",
    )(total, factor)


def solution(mesh):
    in_specs = (P("dp", None, "mp"), P("dp", None, "mp"))
    out_specs = (P("dp", "mp"), P("dp"))
    return jax.shard_map(
        on_device, mesh=mesh, in_specs=in_specs, out_specs=out_specs, check_vma=False
    )
```

```python
import functools
import math

import jax
import jax.numpy as jnp
from jax import lax
from jax.experimental import pallas as pl
from jax.experimental.pallas import tpu as pltpu
from jax.sharding import PartitionSpec as P

D = 2304
F = 18432
SEQ = 256
MESH = pl.DeviceIdType.MESH
NZ = 8
SIDE = 4
OWN = 72
EX = 4
TOK = EX * SEQ
COLS = F // NZ
BOUND = math.sqrt(F * D * SEQ)
PIECES = ((0, 16, 1280), (16, 16, 1024), (32, 16, 1280), (48, 16, 1024), (64, 8, 1280))
TILE = 256
HALF = 160
ORDER = (
    "g10 g21 a010 g20", "a011 x a110 g31", "g30 a020 a021 a111", "g41 g40 a030 a031", "a120 G a040 a041",
    "a121 a130 n a210", "l0 X s0 a211", "m0001 m0012 m0023 a131", "m0034 m0045 a140 m0101", "m0112 a220 m0123 m0134",
    "a141 a221 a310 l1", "s1 m1001 a311 m1012", "m1023 a230 m1034 m1101", "m1112 a231 m1123 m1134", "a320 m1145 r00 a321",
    "r01 a240 a241 a330", "a410 r10 a331 l2", "s2 a411 m2001 m2012", "a340 m2023 m2034 a420", "m2045 m2101 a341 a421",
    "m2112 m2123 m2134 l3", "s3 m3001 a430 m3012", "m3023 a431 m3034 m3101", "m3112 m3123 m3134 a440", "m3145 r11 a441 R00",
    "R01 r20 R10 r21", "l4 s4 m4001 m4012", "m4023 m4034 m4045 m4101", "m4112 m4123 m4134 r30", "R11 r31 R21 R20",
    "r41 r40 R30 R31", "R41 R40",
)
F32, BF16 = jnp.float32, jnp.bfloat16


def tn_dot(a, b):
    return lax.dot_general(a, b, (((0,), (0,)), ((), ())), preferred_element_type=F32)


def nt_dot(a, b):
    return lax.dot_general(a, b, (((1,), (1,)), ((), ())), preferred_element_type=F32)


def kernel(x_hbm, g_hbm, out_hbm, clip_out, *scratch):
    NP = len(PIECES)
    names = iter(scratch)
    acts, graw, gt, clipv, tile, parts, gram, gram_s, gram_r = (next(names) for _ in range(9))
    grads = [next(names) for _ in PIECES]
    peer = [next(names) for _ in PIECES]
    scaled = [next(names) for _ in PIECES]
    part = [next(names) for _ in PIECES]
    send1 = [(next(names), next(names)) for _ in PIECES]
    recv1 = [(next(names), next(names)) for _ in PIECES]
    sums = [(next(names), next(names)) for _ in PIECES]
    recv2 = [(next(names), next(names)) for _ in PIECES]
    far_s = [(next(names), next(names)) for _ in PIECES]
    far_r = [(next(names), next(names)) for _ in PIECES]
    out, local_sem, out_sem, gs_s, gs_r, pair_s, pair_r, ring_s, ring_r, norm_s, norm_r, p1_s, p1_r, p2_s, p2_r = names

    dp, z = lax.axis_index("dp"), lax.axis_index("mp")
    y, x, c = dp // 8, (dp // 2) % SIDE, dp % 2
    other = 1 - c

    def at(y, x, c, z):
        return (y * 8 + x * 2 + c, z)

    def xs(k):
        return lax.rem(x + k, SIDE)

    def ys(k):
        return lax.rem(y + k, SIDE)

    def zs(k):
        return lax.rem(z + k + NZ, NZ)

    peer_id = at(y, x, other, z)
    group = [(dz, dc) for dz in range(NZ) for dc in range(2) if dz or dc]

    def group_id(dz, dc):
        return at(y, x, lax.rem(c + dc, 2), zs(dz))

    load_x = pltpu.make_async_copy(x_hbm, acts.at[pl.ds(c * EX, EX)], local_sem.at[0])
    load_g = pltpu.make_async_copy(g_hbm, graw, local_sem.at[1])
    load_g.start()
    load_x.start()

    barrier = pltpu.get_barrier_semaphore()
    for dz, dc in group:
        pl.semaphore_signal(barrier, inc=1, device_id=group_id(dz, dc), device_id_type=MESH)
    for k in range(1, SIDE):
        pl.semaphore_signal(barrier, inc=1, device_id=at(y, xs(k), c, z), device_id_type=MESH)
        pl.semaphore_signal(barrier, inc=1, device_id=at(ys(k), x, c, z), device_id_type=MESH)

    def remote(src, dst, ssem, rsem, to):
        return pltpu.make_async_remote_copy(
            src_ref=src, dst_ref=dst, send_sem=ssem, recv_sem=rsem, device_id=to, device_id_type=MESH
        )

    begun, arrived = [], set()

    def start(copy, *key):
        copy(*key).start()
        begun.append((copy, key))

    def arrive(copy, *key):
        if (copy, key) not in arrived:
            arrived.add((copy, key))
            incoming.get(copy, copy)(*key).wait_recv()

    def pair_x():
        here = acts.at[pl.ds(c * EX, EX)]
        return remote(here, here, pair_s.at[0], pair_r.at[0], peer_id)


    token0 = pl.multiple_of(c * TOK, TOK)
    token1 = pl.multiple_of(other * TOK, TOK)

    def rows_of(core, first, n):
        return jnp.concatenate(
            [gt[pl.ds(pl.multiple_of(a * 2 * OWN + core * OWN + first, 8), n), :] for a in range(2)], axis=0
        ).astype(BF16)

    def pair_g(p):
        return remote(peer[p], grads[p].at[z, :, pl.ds(token0, TOK)], pair_s.at[1 + p], pair_r.at[1 + p], peer_id)

    def ring(p, s, h, q):
        src = zs(-(h - 1) if s == 0 else h - 1)
        view = grads[p].at[src, :, pl.ds(token0 if q == 0 else token1, TOK)]
        return remote(view, view, ring_s.at[p, s, h - 1, q], ring_r.at[p, s, h - 1, q],
                      at(y, x, c, zs(1 if s == 0 else -1)))

    def ring_in(p, s, h, q):
        src = zs(-h if s == 0 else h)
        view = grads[p].at[src, :, pl.ds(token0 if q == 0 else token1, TOK)]
        return remote(view, view, ring_s.at[p, s, h - 1, q], ring_r.at[p, s, h - 1, q],
                      at(y, x, c, zs(1 if s == 0 else -1)))

    def pair_g_in(p):
        view = grads[p].at[z, :, pl.ds(token1, TOK)]
        return remote(peer[p], view, pair_s.at[1 + p], pair_r.at[1 + p], peer_id)

    def ring_step(p, h, q):
        if h == 1 and q == 1:
            arrive(pair_g, p)
        for s in range(2):
            if h == 4 and s != q:
                arrive(ring, p, s, 3, q)
                continue
            if h > 1:
                arrive(ring, p, s, h - 1, q)
            start(ring, p, s, h, q)

    def ring_last(p):
        for s in range(2):
            arrive(ring, p, s, 4, s)

    def local_gram(e):
        v = acts[c * EX + e]
        for m, g in ((0, nt_dot(v, v)), (1, tn_dot(graw[e], graw[e]))):
            blocks = [g[64 * i:64 * i + 64, 64 * i:64 * i + 128] for i in range(3)]
            blocks.append(jnp.concatenate([g[192:, 192:], g[192:, :64]], axis=1))
            blocks.append(jnp.concatenate([g[:64, 128:192], g[64:128, 192:]], axis=1))
            for i, block in enumerate(blocks):
                row = (2 * e + m) * 40 + 8 * i
                for d in range(NZ):
                    gram[d, row:row + 8] = block[8 * d:8 * d + 8]

    def gram_copy(s, h, late):
        part = pl.ds((s ^ late) * HALF, HALF)
        return remote(gram_s.at[s, h - 1, part], gram_r.at[s, h - 1, part], gs_s.at[s, h - 1, late],
                      gs_r.at[s, h - 1, late], at(y, x, c, zs(1 if s == 0 else -1)))

    def gram_step(h, late):
        for s in range(2):
            d = zs(5 - h if s == 0 else h - 5)
            part = slice((s ^ late) * HALF, ((s ^ late) + 1) * HALF)
            v = gram[d, part]
            if h > 1 + late:
                arrive(gram_copy, s, h - 1, late)
                v = v + gram_r[s, h - 2, part].astype(F32)
            gram_s[s, h - 1, part] = v.astype(BF16)
            start(gram_copy, s, h, late)

    slot = z * 2 + c

    def gram_last():
        for s in range(2):
            arrive(gram_copy, s, 4, 1)
            arrive(gram_copy, s, 4, 0)
        v = gram[z] + gram_r[0, 3].astype(F32) + gram_r[1, 3].astype(F32)
        v = v.reshape(EX, 2, 40, 128)
        w = v[:, 0] * v[:, 1]
        twice = 1.0 + (lax.broadcasted_iota(jnp.int32, (EX, 128), 1) >= 64).astype(F32)
        tile[...] = twice * jnp.sum(w[:, :32], axis=1) + 2.0 * jnp.sum(w[:, 32:], axis=1)
        parts[slot] = tile[...]
        for i in range(len(group)):
            start(norm, i)

    def norm(i):
        dz, dc = group[i]
        return remote(tile, parts.at[slot], norm_s.at[i], norm_r.at[i], group_id(dz, dc))

    def norm_in(i):
        dz, dc = group[i]
        src = lax.rem(z - dz + NZ, NZ) * 2 + lax.rem(c + dc, 2)
        return remote(tile, parts.at[src], norm_s.at[i], norm_r.at[i], group_id(dz, dc))

    def norm_wait():
        for i in range(len(group)):
            arrive(norm, i)
        for core in range(2):
            total = parts[core]
            for zz in range(1, NZ):
                total = total + parts[2 * zz + core]
            total = jnp.sum(total, axis=1, keepdims=True)
            factor = BOUND / jnp.maximum(jnp.sqrt(total), BOUND)
            for e in range(EX):
                b = core * EX + e
                clipv[:, b * SEQ:(b + 1) * SEQ] = jnp.broadcast_to(factor[e:e + 1, :], (1, SEQ))
        for e in range(EX):
            v = clipv[:, pl.ds(pl.multiple_of((c * EX + e) * SEQ, SEQ), 128)]
            clip_out[e] = jnp.max(v)

    def p1(p, half, k):
        to = at(y, xs(k), c, z) if half == 0 else at(ys(k), x, c, z)
        return remote(send1[p][half].at[k - 1], recv1[p][half].at[k - 1],
                      p1_s.at[p, half, k - 1], p1_r.at[p, half, k - 1], to)

    def p2(p, half, k):
        to = at(ys(k), x, c, z) if half == 0 else at(y, xs(k), c, z)
        block = ys(k) if half == 0 else xs(k)
        src, dst = (far_s[p][half], far_r[p][half]) if k == 2 else (sums[p][half].at[block], recv2[p][half].at[k // 2])
        return remote(src, dst, p2_s.at[p, half, k - 1], p2_r.at[p, half, k - 1], to)

    def span(p, half):
        cut = PIECES[p][2]
        return (0, cut) if half == 0 else (cut, COLS - cut)

    def dests(half, k):
        if half == 0:
            return [i * SIDE + xs(k) for i in range(SIDE)]
        return [ys(k) * SIDE + i for i in range(SIDE)]

    def scale(p):
        for zz in range(NZ):
            scaled[p][zz] = (grads[p][zz].astype(F32) * clipv[...]).astype(BF16)

    def multiply(p, half, lo, hi):
        first, n, _ = PIECES[p]
        base, width = span(p, half)

        def body(i, _):
            cols = pl.ds(pl.multiple_of(base + i * TILE, TILE), TILE)
            local = pl.ds(pl.multiple_of(i * TILE, TILE), TILE)
            lhs = scaled[p][...].reshape(NZ * 2 * n, 2 * TOK)
            rhs = acts[:, :, cols].reshape(2 * TOK, TILE)
            part[p][:, :, cols] = jnp.dot(lhs, rhs, preferred_element_type=F32).reshape(16, n, TILE)
            for k in range(1, SIDE):
                v = jnp.concatenate([part[p][j, :, cols] for j in dests(half, k)], axis=0)
                send1[p][half][k - 1, :, local] = v.astype(BF16)
            return 0

        lax.fori_loop(lo, min(hi, width // TILE), body, 0)
        if hi >= width // TILE:
            for k in range(1, SIDE):
                start(p1, p, half, k)

    def reduce1(p, half):
        first, n, _ = PIECES[p]
        base, width = span(p, half)
        for k in range(1, SIDE):
            arrive(p1, p, half, k)

        def body(i, _):
            cols = pl.ds(pl.multiple_of(base + i * TILE, TILE), TILE)
            local = pl.ds(pl.multiple_of(i * TILE, TILE), TILE)
            v = jnp.concatenate([part[p][j, :, cols] for j in dests(half, 0)], axis=0)
            for k in range(1, SIDE):
                v = v + recv1[p][half][k - 1, :, local].astype(F32)
            for i in range(SIDE):
                sums[p][half][i, :, local] = v[i * n:(i + 1) * n]
            return 0

        lax.fori_loop(0, width // TILE, body, 0)
        for k in (1, 3):
            start(p2, p, half, k)
        v = sums[p][half][ys(2) if half == 0 else xs(2)]
        far_s[p][half][...] = jnp.concatenate([v[:, :width // 2], v[:, width // 2:]], axis=0).astype(BF16)
        start(p2, p, half, 2)

    stored = []

    def store(p, half):
        first, n, _ = PIECES[p]
        base, width = span(p, half)
        view = (pl.ds(first, n), pl.ds(base, width))
        return pltpu.make_async_copy(out.at[view], out_hbm.at[view], out_sem.at[p, half])

    def reduce2(p, half):
        first, n, _ = PIECES[p]
        base, width = span(p, half)
        for k in range(1, SIDE):
            arrive(p2, p, half, k)
        v = sums[p][half][y if half == 0 else x] + recv2[p][half][0] + recv2[p][half][1]
        far = far_r[p][half][...].astype(F32)
        v = v + jnp.concatenate([far[:n], far[n:]], axis=1)
        out[first:first + n, base:base + width] = v * (1.0 / 128)
        store(p, half).start()
        stored.append((p, half))

    def pair_x_in():
        return remote(x_hbm, acts.at[pl.ds(other * EX, EX)], pair_s.at[0], pair_r.at[0], peer_id)

    def wait_pair_x():
        arrive(pair_x)

    def begin_pair_x():
        start(pair_x)

    incoming = {pair_x: pair_x_in, pair_g: pair_g_in, ring: ring_in, norm: norm_in}

    load_g.wait()
    for e in range(EX):
        gt[:, e * SEQ:(e + 1) * SEQ] = graw[e].astype(F32)
    for p, (first, n, _) in enumerate(PIECES):
        peer[p][...] = rows_of(other, first, n)
        grads[p][z, :, pl.ds(token0, TOK)] = rows_of(c, first, n)

    load_x.wait()
    for e in range(EX):
        local_gram(e)
    pl.semaphore_wait(barrier, len(group) + 2 * (SIDE - 1))
    for p in range(NP):
        start(pair_g, p)

    steps = {
        "a": ring_step,
        "l": ring_last,
        "g": gram_step,
        "G": gram_last,
        "n": norm_wait,
        "x": begin_pair_x,
        "X": wait_pair_x,
        "s": scale,
        "m": multiply,
        "r": reduce1,
        "R": reduce2,
    }
    for word in " ".join(ORDER).split():
        steps[word[0]](*(int(v) for v in word[1:]))

    for key in stored:
        store(*key).wait()
    for copy, key in begun:
        arrive(copy, *key)
        copy(*key).wait_send()


def hand_on(total, factor, out, clip_out, held, sems):
    def copy(way, i):
        rows = pl.ds(24 * i, 24)
        src, dst = ((total, held), (held, out))[way]
        return pltpu.make_async_copy(src.at[rows], dst.at[rows], sems.at[way, i])

    for i in range(3):
        copy(0, i).start()
    for e in range(EX):
        clip_out[e] = factor[e]
    for i in range(3):
        copy(0, i).wait()
        copy(1, i).start()
    for i in range(3):
        copy(1, i).wait()


def on_device(acts, out_grads):
    np_ = len(PIECES)
    dma = pltpu.SemaphoreType.DMA
    scratch = [
        pltpu.VMEM((2 * EX, SEQ, COLS), BF16),
        pltpu.VMEM((EX, D // NZ, SEQ), BF16),
        pltpu.VMEM((D // NZ, TOK), F32),
        pltpu.VMEM((1, 2 * TOK), F32),
        pltpu.VMEM((EX, 128), F32),
        pltpu.VMEM((2 * NZ, EX, 128), F32),
        pltpu.VMEM((NZ, 2 * HALF, 128), F32),
        pltpu.VMEM((2, 4, 2 * HALF, 128), BF16),
        pltpu.VMEM((2, 4, 2 * HALF, 128), BF16),
    ]
    widths = [((0, cut), (1, COLS - cut)) for _, _, cut in PIECES]
    scratch += [pltpu.VMEM((NZ, 2 * n, 2 * TOK), BF16) for _, n, _ in PIECES]
    scratch += [pltpu.VMEM((2 * n, TOK), BF16) for _, n, _ in PIECES]
    scratch += [pltpu.VMEM((NZ, 2 * n, 2 * TOK), BF16) for _, n, _ in PIECES]
    scratch += [pltpu.VMEM((16, n, COLS), F32) for _, n, _ in PIECES]
    for shape in ("send", "recv"):
        scratch += [
            pltpu.VMEM((3, 4 * n, w), BF16) for (_, n, cut) in PIECES for w in (cut, COLS - cut)
        ]
    scratch += [pltpu.VMEM((4, n, w), F32) for (_, n, cut) in PIECES for w in (cut, COLS - cut)]
    scratch += [pltpu.VMEM((2, n, w), F32) for (_, n, cut) in PIECES for w in (cut, COLS - cut)]
    for shape in ("send", "recv"):
        scratch += [pltpu.VMEM((2 * n, w // 2), BF16) for (_, n, cut) in PIECES for w in (cut, COLS - cut)]
    scratch += [
        pltpu.VMEM((OWN, COLS), F32),
        dma((2,)),
        dma((np_, 2)),
        dma((2, 4, 2)),
        dma((2, 4, 2)),
        dma((1 + np_,)),
        dma((1 + np_,)),
        dma((np_, 2, 4, 2)),
        dma((np_, 2, 4, 2)),
        dma((15,)),
        dma((15,)),
        dma((np_, 2, 3)),
        dma((np_, 2, 3)),
        dma((np_, 2, 3)),
        dma((np_, 2, 3)),
    ]
    total, factor = pl.pallas_call(
        kernel,
        out_shape=(
            jax.ShapeDtypeStruct((OWN, COLS), F32),
            jax.ShapeDtypeStruct((EX,), F32),
        ),
        in_specs=[pl.BlockSpec(memory_space=pl.ANY)] * 2,
        out_specs=(pl.BlockSpec(memory_space=pl.ANY), pl.BlockSpec(memory_space=pltpu.SMEM)),
        scratch_shapes=scratch,
        compiler_params=pltpu.CompilerParams(
            collective_id=0, has_side_effects=True, vmem_limit_bytes=60 * 2**20
        ),
        name="clipped_grad",
    )(acts, jnp.swapaxes(out_grads, 1, 2))
    return pl.pallas_call(
        hand_on,
        out_shape=(
            jax.ShapeDtypeStruct((OWN, COLS), F32),
            jax.ShapeDtypeStruct((EX,), F32),
        ),
        in_specs=[pl.BlockSpec(memory_space=pl.ANY), pl.BlockSpec(memory_space=pltpu.SMEM)],
        out_specs=(pl.BlockSpec(memory_space=pl.ANY), pl.BlockSpec(memory_space=pltpu.SMEM)),
        scratch_shapes=[pltpu.VMEM((OWN, COLS), F32), dma((2, 3))],
        name="hand_on",
    )(total, factor)


def solution(mesh):
    in_specs = (P("dp", None, "mp"), P("dp", None, "mp"))
    out_specs = (P("dp", "mp"), P("dp"))
    return jax.shard_map(
        on_device, mesh=mesh, in_specs=in_specs, out_specs=out_specs, check_vma=False
    )
```
